768 devices in a mesh: row: 16 (over z_hi, x), col: 8 (over y), depth: 6 (over z_lo, core).
Axes of the slice: x: 4, y: 8, z: 12 (z_hi: 4, z_lo: 3; z = z_hi * 3 + z_lo), core: 2. Of those that a mesh axis runs over, the one named last changes fastest.
Arguments:
- left_panels: bfloat16 [8192, 6, 2048], P('row', 'depth', 'col'), may hold values from -6 to 6
- right_panels: bfloat16 [6, 2048, 6144], P('depth', 'row', 'col'), may hold values from -0.0546875 to 0.0546875
- left_flags: int32 [64, 6, 16], P('row', 'depth', 'col'), may hold values from 0 to 1, as said below
- right_flags: int32 [6, 16, 48], P('depth', 'row', 'col'), may hold values 0 or 1
- target_flags: int32 [64, 48], P('row', ('col', 'depth')), may hold values 0 or 1
Outputs:
- product: bfloat16 [8192, 6144], P('row', ('col', 'depth'))
The draws below stay inside these ranges and needn't reach their ends.
Inputs may be any that keep to these rules, and one draw needn't show every extreme that they name: `left_flags`: 1 where the block is stored, else 0.
All inputs are finite; a program needn't handle non-finite values. No bound on the sum of `right_flags` or of `target_flags` on one device may be relied on, other than what follows from the above.
Results may differ from the reference program's by a relative error of at most 0.001.
Values may be sent and summed in bfloat16 or wider, within the bound.
A program may use at most 32 MiB of HBM per device.

```python
import jax
import jax.numpy as jnp
from jax import lax

BLOCK = 128
LAYERS = 6
MBLK = 64
KBLK = 16
NBLK = 48
M = 8192
KSLAB = 2048
N = 6144


def draw_left_flags(key, part):
    key = jax.random.fold_in(key, 11)
    levels = jax.random.randint(key, (MBLK, LAYERS, KBLK), 0, 100)
    row_index = lax.broadcasted_iota(jnp.int32, (MBLK, LAYERS, KBLK), 0)
    bounds = 20 + 75 * row_index // max(MBLK - 1, 1)
    return (levels < bounds).astype(jnp.int32)


def plant(result, stream_key, low, largest):
    longest = result.shape.index(max(result.shape))
    spots = []
    for shift in (0, 1):
        where = [jax.random.randint(jax.random.fold_in(stream_key, axis), (), 0, length) for axis, length in enumerate(result.shape)]
        where[longest] = (where[longest] + shift) % result.shape[longest]
        spots.append(tuple(where))
    return result.at[spots[0]].set(low).at[spots[1]].set(largest)


def shard_levels(own_key, shape, cuts, low, top_value):
    level, own = 1.0, jax.random.fold_in(own_key, 6)
    for position, blocks in cuts:
        steps = jnp.exp(jax.random.uniform(jax.random.fold_in(own, position), (blocks,), jnp.float32, low / len(cuts), top_value / len(cuts)))
        level = level * jnp.repeat(steps, shape[position] // blocks).reshape([-1 if axis == position else 1 for axis in range(len(shape))])
    return level


def centred(stream_key, extent, deviation, reach, split=(), kind=jnp.bfloat16):
    drawn = jax.random.normal(stream_key, extent, jnp.float32) * deviation
    if len(split) > 0:
        drawn = shard_levels(stream_key, extent, split, -0.22, 0.18) * drawn
    return jnp.clip(drawn, min=-reach, max=reach).astype(kind)


def setup_inputs(seed: int = 0) -> dict:
    splits = jax.random.split(jax.random.key(seed), 6)
    left_panels = centred(splits[0], (M, LAYERS, KSLAB), 1.0, 6.0, ((0, 16), (1, 6), (2, 8)))
    right_panels = centred(splits[1], (LAYERS, KSLAB, N), (KSLAB * LAYERS) ** -0.5, 0.0546875, ((0, 6), (1, 16), (2, 8)))
    left_flags = draw_left_flags(jax.random.fold_in(splits[5], 71), 0)
    right_flags = plant((jax.random.randint(splits[3], (LAYERS, KBLK, NBLK), 0, 3) < 2).astype(jnp.int32), jax.random.fold_in(splits[3], 1), 0, 1)
    target_flags = plant((jax.random.randint(splits[4], (MBLK, NBLK), 0, 4) < 3).astype(jnp.int32), jax.random.fold_in(splits[4], 1), 0, 1)
    return dict(left_panels=left_panels, right_panels=right_panels, left_flags=left_flags, right_flags=right_flags, target_flags=target_flags)


def spread(occupancy, out_type):
    height, breadth = occupancy.shape
    expanded = jnp.broadcast_to(occupancy[:, None, :, None], (height, BLOCK, breadth, BLOCK))
    return expanded.reshape(height * BLOCK, breadth * BLOCK).astype(out_type)


def reference(left_panels, right_panels, left_flags, right_flags, target_flags):
    accumulated = jnp.zeros((M, N), jnp.float32)
    for layer_index in range(LAYERS):
        left_masked = left_panels[:, layer_index, :] * spread(left_flags[:, layer_index, :], jnp.bfloat16)
        right_masked = right_panels[layer_index] * spread(right_flags[layer_index], jnp.bfloat16)
        accumulated = accumulated + jnp.dot(left_masked, right_masked, preferred_element_type=jnp.float32)
    return (accumulated * spread(target_flags, jnp.float32)).astype(jnp.bfloat16)
```

```python
import jax
import jax.numpy as jnp
from jax import lax
from jax.experimental import pallas as pl
from jax.experimental.pallas import tpu as pltpu
from jax.sharding import PartitionSpec as P

BLOCK = 128
MESH = pl.DeviceIdType.MESH
NX, NY, NZH, NZL = 4, 8, 4, 3
HALF = 256
WIDE = 256
CHUNKS = 3


def kernel(
    left_hbm, right_hbm, left_flags, right_flags, target_flags, out_ref,
    left_in, right_in, left_buf, right_buf, part, sib_recv, red_send, red_recv,
    in_sem, left_send, left_recv, z_send, z_recv, x_send, x_recv,
    sib_send_sem, sib_recv_sem, red_send_sem, red_recv_sem,
):
    row, col, depth = lax.axis_index("row"), lax.axis_index("col"), lax.axis_index("depth")
    zh, x = row // NX, row % NX
    zl, core = depth // 2, depth % 2
    sign = 1 - 2 * core

    def y_id(step):
        return (row, (col + step * sign + NY) % NY, depth)

    def x_id(step):
        return (zh * NX + (x + step * sign + NX) % NX, col, depth)

    def z_id(step):
        return (((zh + step * sign + NZH) % NZH) * NX + x, col, depth)

    def layer_id(step):
        return (row, col, ((zl + step) % NZL) * 2 + core)

    sibling = (row, col, zl * 2 + 1 - core)

    left_copy = pltpu.make_async_copy(left_hbm, left_in, in_sem.at[0])
    right_copy = pltpu.make_async_copy(right_hbm, right_in, in_sem.at[1])
    left_copy.start()
    right_copy.start()

    barrier = pltpu.get_barrier_semaphore()
    friends = [y_id(1), y_id(-1), x_id(1), x_id(-1), z_id(1), z_id(-1), layer_id(1), layer_id(2), sibling]
    for friend in friends:
        pl.semaphore_signal(barrier, inc=1, device_id=friend, device_id_type=MESH)

    def chunk_of(step):
        return (zl + 1 + step) % NZL

    def mask_left(half):
        for block in range(2):
            rows = pl.ds(half * HALF + block * BLOCK, BLOCK)
            for k in range(2):
                columns = pl.ds(k * BLOCK, BLOCK)
                keep = left_flags[k, half * 2 + block] > 0
                value = left_in[rows, columns]
                left_buf[col, rows, columns] = jnp.where(keep, value, jnp.zeros_like(value))

    def mask_right(step):
        chunk = chunk_of(step)
        for j in range(2):
            keep = right_flags[0, chunk * 2 + j] > 0
            start = pl.multiple_of(chunk * WIDE + j * BLOCK, BLOCK)
            value = right_in[:, pl.ds(start, BLOCK)]
            right_buf[step, row, :, pl.ds(j * BLOCK, BLOCK)] = jnp.where(keep, value, jnp.zeros_like(value))

    pending = []

    def send(ref, send_sem, recv_sem, target):
        copy = pltpu.make_async_remote_copy(
            src_ref=ref, dst_ref=ref, send_sem=send_sem, recv_sem=recv_sem,
            device_id=target, device_id_type=MESH,
        )
        copy.start()
        pending.append(copy)

    def arrived(ref, send_sem, recv_sem, target):
        pltpu.make_async_remote_copy(
            src_ref=ref, dst_ref=ref, send_sem=send_sem, recv_sem=recv_sem,
            device_id=target, device_id_type=MESH,
        ).wait_recv()

    def left_ref(hop, way, half):
        shift = -hop * sign if way == 0 else hop * sign
        return left_buf.at[(col + shift + NY) % NY, pl.ds(half * HALF, HALF), :]

    def left_send_hop(hop, way, half):
        send(left_ref(hop - 1, way, half), left_send.at[hop - 1, way, half],
             left_recv.at[hop - 1, way, half], y_id(1 if way == 0 else -1))

    def left_wait(hop, way, half):
        arrived(left_ref(hop, way, half), left_send.at[hop - 1, way, half],
                left_recv.at[hop - 1, way, half], y_id(1 if way == 0 else -1))

    def left_event(hop, half):
        left_wait(hop, 0, half)
        if hop < 4:
            left_send_hop(hop + 1, 0, half)
        if hop < 4:
            left_wait(hop, 1, half)
            if hop < 3:
                left_send_hop(hop + 1, 1, half)

    def zh_of(kind):
        shift = (0, -sign, sign, 2)[kind]
        return (zh + shift + NZH) % NZH

    def z_ref(step, kind):
        return right_buf.at[step, zh_of(kind) * NX + x]

    def z_start(step):
        send(z_ref(step, 0), z_send.at[step, 0], z_recv.at[step, 0], z_id(1))
        send(z_ref(step, 0), z_send.at[step, 1], z_recv.at[step, 1], z_id(-1))

    def z_first(step):
        arrived(z_ref(step, 1), z_send.at[step, 0], z_recv.at[step, 0], z_id(1))
        send(z_ref(step, 1), z_send.at[step, 2], z_recv.at[step, 2], z_id(1))
        x_start(step, 1)
        arrived(z_ref(step, 2), z_send.at[step, 1], z_recv.at[step, 1], z_id(-1))
        x_start(step, 2)

    def z_second(step):
        arrived(z_ref(step, 3), z_send.at[step, 2], z_recv.at[step, 2], z_id(1))
        x_start(step, 3)

    def x_ref(step, kind, shift):
        return right_buf.at[step, zh_of(kind) * NX + (x + shift * sign + NX) % NX]

    def x_start(step, kind):
        send(x_ref(step, kind, 0), x_send.at[step, kind, 0], x_recv.at[step, kind, 0], x_id(1))
        send(x_ref(step, kind, 0), x_send.at[step, kind, 1], x_recv.at[step, kind, 1], x_id(-1))

    def x_first(step, kind):
        arrived(x_ref(step, kind, -1), x_send.at[step, kind, 0], x_recv.at[step, kind, 0], x_id(1))
        send(x_ref(step, kind, -1), x_send.at[step, kind, 2], x_recv.at[step, kind, 2], x_id(1))

    def x_last(step):
        for kind in range(4):
            arrived(x_ref(step, kind, 1), x_send.at[step, kind, 1], x_recv.at[step, kind, 1], x_id(-1))
        for kind in range(4):
            arrived(x_ref(step, kind, 2), x_send.at[step, kind, 2], x_recv.at[step, kind, 2], x_id(1))

    def multiply(step):
        total = None
        for k in range(NY):
            term = jnp.dot(
                left_buf[k], right_buf[step, 2 * k:2 * k + 2].reshape(2 * BLOCK, WIDE),
                preferred_element_type=jnp.float32,
            )
            total = term if total is None else total + term
        part[step, 0] = total[:, :BLOCK]
        part[step, 1] = total[:, BLOCK:]
        copy = pltpu.make_async_remote_copy(
            src_ref=part.at[step, 1 - core], dst_ref=sib_recv.at[step],
            send_sem=sib_send_sem.at[step], recv_sem=sib_recv_sem.at[step],
            device_id=sibling, device_id_type=MESH,
        )
        copy.start()
        pending.append(copy)
        return copy

    def reduce_send(step, copy):
        copy.wait_recv()
        red_send[step] = part[step, core] + sib_recv[step]
        copy = pltpu.make_async_remote_copy(
            src_ref=red_send.at[step], dst_ref=red_recv.at[step],
            send_sem=red_send_sem.at[step], recv_sem=red_recv_sem.at[step],
            device_id=layer_id(1 + step), device_id_type=MESH,
        )
        copy.start()
        pending.append(copy)
        return copy

    right_copy.wait()
    mask_right(0)
    left_copy.wait()
    mask_left(0)
    pl.semaphore_wait(barrier, len(friends))
    z_start(0)
    x_start(0, 0)
    left_send_hop(1, 0, 0)
    left_send_hop(1, 1, 0)
    mask_left(1)
    left_send_hop(1, 0, 1)
    left_send_hop(1, 1, 1)
    mask_right(1)
    z_start(1)
    x_start(1, 0)
    mask_right(2)
    x_start(2, 0)

    x_first(0, 0)
    left_event(1, 0)
    z_first(0)
    z_start(2)
    x_first(1, 0)
    x_first(2, 0)
    left_event(1, 1)
    x_first(0, 1)
    x_first(0, 2)
    left_event(2, 0)
    z_first(1)
    z_second(0)
    left_event(2, 1)
    x_first(1, 1)
    x_first(1, 2)
    x_first(0, 3)
    left_event(3, 0)
    z_first(2)
    left_event(3, 1)
    z_second(1)
    x_first(2, 1)
    x_first(2, 2)
    x_first(1, 3)
    z_second(2)
    left_event(4, 0)
    left_event(4, 1)
    x_last(0)
    first = multiply(0)
    x_first(2, 3)
    red0 = reduce_send(0, first)
    x_last(1)
    second = multiply(1)
    red1 = reduce_send(1, second)
    x_last(2)
    third = multiply(2)
    third.wait_recv()
    total = part[2, core] + sib_recv[2]
    red0.wait_recv()
    red1.wait_recv()
    total = total + red_recv[0] + red_recv[1]
    for block in range(4):
        rows = slice(block * BLOCK, (block + 1) * BLOCK)
        keep = target_flags[0, block] > 0
        value = total[rows]
        out_ref[rows, :] = jnp.where(keep, value, jnp.zeros_like(value)).astype(jnp.bfloat16)
    for copy in pending:
        copy.wait_send()


def on_device(left_panels, right_panels, left_flags, right_flags, target_flags):
    dma = pltpu.SemaphoreType.DMA
    return pl.pallas_call(
        kernel,
        out_shape=jax.ShapeDtypeStruct((4 * BLOCK, BLOCK), jnp.bfloat16),
        in_specs=[pl.BlockSpec(memory_space=pl.ANY)] * 2 + [pl.BlockSpec(memory_space=pltpu.SMEM)] * 3,
        out_specs=pl.BlockSpec(memory_space=pltpu.VMEM),
        scratch_shapes=[
            pltpu.VMEM((4 * BLOCK, 2 * BLOCK), jnp.bfloat16),
            pltpu.VMEM((BLOCK, 6 * BLOCK), jnp.bfloat16),
            pltpu.VMEM((NY, 4 * BLOCK, 2 * BLOCK), jnp.bfloat16),
            pltpu.VMEM((CHUNKS, NX * NZH, BLOCK, WIDE), jnp.bfloat16),
            pltpu.VMEM((CHUNKS, 2, 4 * BLOCK, BLOCK), jnp.float32),
            pltpu.VMEM((CHUNKS, 4 * BLOCK, BLOCK), jnp.float32),
            pltpu.VMEM((2, 4 * BLOCK, BLOCK), jnp.float32),
            pltpu.VMEM((2, 4 * BLOCK, BLOCK), jnp.float32),
            dma((2,)),
            dma((4, 2, 2)),
            dma((4, 2, 2)),
            dma((CHUNKS, 3)),
            dma((CHUNKS, 3)),
            dma((CHUNKS, 4, 3)),
            dma((CHUNKS, 4, 3)),
            dma((CHUNKS,)),
            dma((CHUNKS,)),
            dma((2,)),
            dma((2,)),
        ],
        compiler_params=pltpu.CompilerParams(
            collective_id=0, has_side_effects=True, vmem_limit_bytes=32 * 1024 * 1024
        ),
        cost_estimate=pl.CostEstimate(flops=1_610_612_736, bytes_accessed=600_000, transcendentals=0),
    )(left_panels[:, 0, :], right_panels[0], left_flags[:, 0, :].T, right_flags[0], target_flags.T)


def solution(mesh):
    in_specs = (
        P("row", "depth", "col"),
        P("depth", "row", "col"),
        P("row", "depth", "col"),
        P("depth", "row", "col"),
        P("row", ("col", "depth")),
    )
    out_specs = P("row", ("col", "depth"))
    return jax.shard_map(
        on_device, mesh=mesh, in_specs=in_specs, out_specs=out_specs, check_vma=False
    )
```

```python
import jax
import jax.numpy as jnp
from jax import lax
from jax.experimental import pallas as pl
from jax.experimental.pallas import tpu as pltpu
from jax.sharding import PartitionSpec as P

BLOCK = 128
MESH = pl.DeviceIdType.MESH
NX, NY, NZH, NZL = 4, 8, 4, 3
HALF = 256
WIDE = 256
CHUNKS = 3
PARTS = 2

ORDERS = (
    (
        "up 0", "down 0", "own_x 0", "own_left 0", "up 1", "down 1", "own_left 1", "own_x 1",
        "own_x 2", "own_x 3", "own_x 4", "own_x 5", "X 0 0", "X 1 0", "X 2 0", "X 3 0",
        "Zp 0", "up 2", "X 4 0", "Zm 0", "down 2", "L 1 0", "X 5 0", "Zp 1",
        "up 3", "Zm 1", "down 3", "L 1 1", "X 0 1", "X 0 2", "Zo 0", "X 1 1",
        "L 2 0", "X 1 2", "Zp 2", "up 4", "Zm 2", "down 4", "X 0 3", "L 2 1",
        "Zo 1", "Zp 3", "up 5", "Zm 3", "down 5", "X 2 1", "X 2 2", "L 3 0",
        "X 1 3", "X 3 1", "Zp 4", "Zm 4", "X 3 2", "Zo 2", "L 3 1", "Zm 5",
        "Zp 5", "Zo 3", "X 4 1", "X 4 2", "X 2 3", "left_last", "x_last 0", "M 0",
        "X 5 2", "X 5 1", "Zo 4", "X 3 3", "R 0", "Zo 5", "x_last 1", "M 1",
        "X 4 3", "X 5 3", "R 1",
    ),
)


def kernel(
    left_hbm, right_hbm, left_flags, right_flags, target_flags, out_ref,
    left_in, right_in, left_buf, right_buf, part, sib_recv, red_send, red_recv,
    in_sem, left_send, left_recv, left_last, z_send, z_recv, x_send, x_recv, x_last,
    sib_send_sem, sib_recv_sem, red_send_sem, red_recv_sem,
):
    row, col, depth = lax.axis_index("row"), lax.axis_index("col"), lax.axis_index("depth")
    zh, x = row // NX, row % NX
    zl, core = depth // 2, depth % 2
    sign = 1 - 2 * core

    left_copy = pltpu.make_async_copy(left_hbm, left_in, in_sem.at[0])
    right_copy = pltpu.make_async_copy(right_hbm, right_in, in_sem.at[1])
    right_copy.start()
    left_copy.start()

    y_slot = {k: (col + k * sign + NY) % NY for k in range(-4, 4)}
    x_slot = {k: (x + k * sign + NX) % NX for k in (-1, 0, 1, 2)}
    zh_slot = {0: zh, 1: (zh + 3) % NZH, 2: (zh + 1) % NZH, 3: (zh + 2) % NZH}
    y_id = {k: (row, y_slot[k], depth) for k in (1, -1)}
    x_id = {k: (zh * NX + x_slot[k], col, depth) for k in (1, -1)}
    up_id = (zh_slot[2] * NX + x, col, depth)
    down_id = (zh_slot[1] * NX + x, col, depth)
    layer_id = {k: (row, col, ((zl + k) % NZL) * 2 + core) for k in (1, 2)}
    sibling = (row, col, zl * 2 + 1 - core)
    chunk = {k: (zl + 1 + k) % NZL for k in range(CHUNKS)}

    barrier = pltpu.get_barrier_semaphore()

    def greet(friend):
        pl.semaphore_signal(barrier, inc=1, device_id=friend, device_id_type=MESH)

    def mask_left():
        for block in range(4):
            rows = pl.ds(block * BLOCK, BLOCK)
            for k in range(2):
                columns = pl.ds(k * BLOCK, BLOCK)
                keep = left_flags[k, block] > 0
                value = left_in[rows, columns]
                left_buf[col, rows, columns] = jnp.where(keep, value, jnp.zeros_like(value))

    def mask_right(step):
        for j in range(2):
            keep = right_flags[0, chunk[step] * 2 + j] > 0
            start = pl.multiple_of(chunk[step] * WIDE + j * BLOCK, BLOCK)
            value = right_in[:, pl.ds(start, BLOCK)]
            right_buf[step, row, :, pl.ds(j * BLOCK, BLOCK)] = jnp.where(keep, value, jnp.zeros_like(value))

    def copy_of(ref, send_sem, recv_sem, target, dst=None):
        return pltpu.make_async_remote_copy(
            src_ref=ref, dst_ref=ref if dst is None else dst, send_sem=send_sem, recv_sem=recv_sem,
            device_id=target, device_id_type=MESH,
        )

    def left_copy_of(hop, way, half, shift):
        slot = y_slot[-shift] if way == 0 else y_slot[shift]
        final = hop == 4 - way
        return copy_of(
            left_buf.at[slot, pl.ds(half * HALF, HALF), :], left_send,
            left_last if final else left_recv.at[hop - 1, way, half], y_id[1 if way == 0 else -1],
        )

    def own_left(half):
        left_copy_of(1, 0, half, 0).start()
        left_copy_of(1, 1, half, 0).start()

    def left_event(hop, half):
        for way in range(2):
            if hop < 4 - way:
                left_copy_of(hop, way, half, hop).wait_recv()
                left_copy_of(hop + 1, way, half, hop).start()

    def z_copy(piece, source, arrival, target):
        rows = pl.ds(piece % PARTS * (BLOCK // PARTS), BLOCK // PARTS)
        ref = right_buf.at[piece // PARTS, zh_slot[source] * NX + x, rows]
        return copy_of(ref, z_send.at[piece // PARTS], z_recv.at[piece, arrival], target)

    def up(piece):
        z_copy(piece, 0, 0, up_id).start()

    def down(piece):
        z_copy(piece, 0, 1, down_id).start()

    def z_from_before(piece):
        z_copy(piece, 1, 0, up_id).wait_recv()

        @pl.when(core == 0)
        def _():
            z_copy(piece, 1, 2, up_id).start()

        own_x(piece, 1)

    def z_from_after(piece):
        z_copy(piece, 2, 1, down_id).wait_recv()

        @pl.when(core == 1)
        def _():
            z_copy(piece, 2, 2, down_id).start()

        own_x(piece, 2)

    def z_opposite(piece):
        z_copy(piece, 3, 2, up_id).wait_recv()
        own_x(piece, 3)

    def x_copy(piece, source, shift, recv_sem, way):
        rows = pl.ds(piece % PARTS * (BLOCK // PARTS), BLOCK // PARTS)
        ref = right_buf.at[piece // PARTS, zh_slot[source] * NX + x_slot[shift], rows]
        return copy_of(ref, x_send.at[piece // PARTS], recv_sem, x_id[way])

    def own_x(piece, source=0):
        x_copy(piece, source, 0, x_recv.at[piece, source], 1).start()
        x_copy(piece, source, 0, x_last.at[piece // PARTS], -1).start()

    def x_event(piece, source):
        x_copy(piece, source, -1, x_recv.at[piece, source], 1).wait_recv()
        x_copy(piece, source, -1, x_last.at[piece // PARTS], 1).start()

    def wait_x_last(step):
        blocks = right_buf.at[step, pl.ds(0, 8)]
        copy_of(blocks, x_send.at[step], x_last.at[step], x_id[1]).wait_recv()

    def wait_left_last():
        copy_of(left_buf.at[pl.ds(0, 2)], left_send, left_last, y_id[1]).wait_recv()

    def sibling_copy(step):
        return copy_of(part.at[step, 1 - core], sib_send_sem.at[step], sib_recv_sem.at[step], sibling, sib_recv.at[step])

    def layer_copy(step):
        return copy_of(red_send.at[step], red_send_sem.at[step], red_recv_sem.at[step], layer_id[1 + step], red_recv.at[step])

    def multiply(step):
        total = None
        for k in range(NY):
            term = jnp.dot(
                left_buf[k], right_buf[step, 2 * k:2 * k + 2].reshape(2 * BLOCK, WIDE),
                preferred_element_type=jnp.float32,
            )
            total = term if total is None else total + term
        part[step, 0] = total[:, :BLOCK]
        part[step, 1] = total[:, BLOCK:]
        sibling_copy(step).start()

    def reduce_send(step):
        sibling_copy(step).wait_recv()
        red_send[step] = part[step, core] + sib_recv[step]
        layer_copy(step).start()

    actions = {
        "own_x": own_x, "own_left": own_left, "X": x_event, "L": left_event, "up": up, "down": down, "Zp": z_from_before,
        "Zm": z_from_after, "Zo": z_opposite, "x_last": wait_x_last, "left_last": wait_left_last, "M": multiply,
        "R": reduce_send,
    }

    def perform(order):
        for item in order:
            name, *numbers = item.split()
            actions[name](*map(int, numbers))

    for friend in (y_id[1], y_id[-1], x_id[1], x_id[-1], sibling):
        greet(friend)
    right_copy.wait()
    for step in range(CHUNKS):
        mask_right(step)
    left_copy.wait()
    mask_left()
    for friend in (layer_id[1], layer_id[2], up_id, down_id):
        greet(friend)
    pl.semaphore_wait(barrier, 9)

    perform(ORDERS[0])

    copy_of(left_buf.at[pl.ds(0, 7)], left_send, left_last, y_id[1]).wait_send()
    for step in range(CHUNKS):
        copy_of(right_buf.at[step, pl.ds(0, 3)], z_send.at[step], z_recv.at[PARTS * step, 0], up_id).wait_send()
    for step in range(CHUNKS):
        copy_of(right_buf.at[step, pl.ds(0, 12)], x_send.at[step], x_last.at[step], x_id[1]).wait_send()
    wait_x_last(2)
    multiply(2)
    sibling_copy(0).wait_send()
    sibling_copy(1).wait_send()
    layer_copy(0).wait()
    layer_copy(1).wait()
    total = part[2, core] + red_recv[0] + red_recv[1]
    sibling_copy(2).wait()
    total = total + sib_recv[2]
    for block in range(4):
        rows = slice(block * BLOCK, (block + 1) * BLOCK)
        keep = target_flags[0, block] > 0
        value = total[rows]
        out_ref[rows, :] = jnp.where(keep, value, jnp.zeros_like(value)).astype(jnp.bfloat16)


def on_device(left_panels, right_panels, left_flags, right_flags, target_flags):
    dma = pltpu.SemaphoreType.DMA
    return pl.pallas_call(
        kernel,
        out_shape=jax.ShapeDtypeStruct((4 * BLOCK, BLOCK), jnp.bfloat16),
        in_specs=[pl.BlockSpec(memory_space=pl.ANY)] * 2 + [pl.BlockSpec(memory_space=pltpu.SMEM)] * 3,
        out_specs=pl.BlockSpec(memory_space=pltpu.VMEM),
        scratch_shapes=[
            pltpu.VMEM((4 * BLOCK, 2 * BLOCK), jnp.bfloat16),
            pltpu.VMEM((BLOCK, 6 * BLOCK), jnp.bfloat16),
            pltpu.VMEM((NY, 4 * BLOCK, 2 * BLOCK), jnp.bfloat16),
            pltpu.VMEM((CHUNKS, NX * NZH, BLOCK, WIDE), jnp.bfloat16),
            pltpu.VMEM((CHUNKS, 2, 4 * BLOCK, BLOCK), jnp.float32),
            pltpu.VMEM((CHUNKS, 4 * BLOCK, BLOCK), jnp.float32),
            pltpu.VMEM((2, 4 * BLOCK, BLOCK), jnp.float32),
            pltpu.VMEM((2, 4 * BLOCK, BLOCK), jnp.float32),
            dma((2,)),
            dma,
            dma((3, 2, 2)),
            dma,
            dma((CHUNKS,)),
            dma((CHUNKS * PARTS, 3)),
            dma((CHUNKS,)),
            dma((CHUNKS * PARTS, 4)),
            dma((CHUNKS,)),
            dma((CHUNKS,)),
            dma((CHUNKS,)),
            dma((2,)),
            dma((2,)),
        ],
        compiler_params=pltpu.CompilerParams(
            collective_id=0, has_side_effects=True, vmem_limit_bytes=VMEM_LIMIT
        ),
        cost_estimate=pl.CostEstimate(flops=1_610_612_736, bytes_accessed=600_000, transcendentals=0),
    )(left_panels[:, 0, :], right_panels[0], left_flags[:, 0, :].T, right_flags[0], target_flags.T)


VMEM_LIMIT = 63 * 1024 * 1024


def solution(mesh):
    in_specs = (
        P("row", "depth", "col"),
        P("depth", "row", "col"),
        P("row", "depth", "col"),
        P("depth", "row", "col"),
        P("row", ("col", "depth")),
    )
    out_specs = P("row", ("col", "depth"))
    return jax.shard_map(
        on_device, mesh=mesh, in_specs=in_specs, out_specs=out_specs, check_vma=False
    )
```

```python
import jax
import jax.numpy as jnp
from jax import lax
from jax.experimental import pallas as pl
from jax.experimental.pallas import tpu as pltpu
from jax.sharding import PartitionSpec as P

BLOCK = 128
MESH = pl.DeviceIdType.MESH
NX, NY, NZH, NZL = 4, 8, 4, 3
HALF = 256
WIDE = 256
CHUNKS = 3
PARTS = 2

ORDERS = (
    (
        "up 0", "down 0", "own_x 0", "own_left 0", "up 1", "down 1", "own_left 1", "own_x 1",
        "own_x 2", "own_x 3", "own_x 4", "own_x 5", "X 0 0", "X 1 0", "X 2 0", "X 3 0",
        "Zp 0", "up 2", "X 4 0", "Zm 0", "down 2", "L 1 0", "X 5 0", "Zp 1",
        "up 3", "Zm 1", "down 3", "L 1 1", "X 0 1", "X 0 2", "Zo 0", "X 1 1",
        "L 2 0", "X 1 2", "Zp 2", "Zo 1", "Zm 2", "up 4", "down 4", "X 0 3",
        "L 2 1", "Zp 3", "up 5", "Zm 3", "down 5", "X 2 1", "X 2 2", "L 3 0",
        "X 1 3", "X 3 1", "Zp 4", "Zm 4", "Zo 3", "X 3 2", "L 3 1", "Zm 5",
        "Zo 2", "Zp 5", "X 4 1", "X 4 2", "X 2 3", "left_last", "x_last 0", "M 0",
        "Zo 4", "X 5 2", "X 5 1", "X 3 3", "R 0", "x_last 1", "M 1", "Zo 5",
        "X 4 3", "X 5 3", "R 1",
    ),
)


def kernel(
    left_hbm, right_hbm, left_flags_hbm, right_flags_hbm, target_flags_hbm, out_ref,
    left_flags, right_flags, target_flags,
    left_in, right_in, left_buf, right_buf, part, sib_recv, red_send, red_recv,
    in_sem, left_send, left_recv, left_last, z_send, z_recv, x_send, x_recv, x_last,
    sib_send_sem, sib_recv_sem, red_send_sem, red_recv_sem,
):
    row, col, depth = lax.axis_index("row"), lax.axis_index("col"), lax.axis_index("depth")
    zh, x = row // NX, row % NX
    zl, core = depth // 2, depth % 2
    sign = 1 - 2 * core

    left_copy = pltpu.make_async_copy(left_hbm, left_in, in_sem.at[0])
    right_copy = pltpu.make_async_copy(right_hbm, right_in, in_sem.at[1])
    flag_copies = [
        pltpu.make_async_copy(right_flags_hbm, right_flags, in_sem.at[2]),
        pltpu.make_async_copy(left_flags_hbm, left_flags, in_sem.at[3]),
        pltpu.make_async_copy(target_flags_hbm, target_flags, in_sem.at[4]),
    ]
    right_copy.start()
    flag_copies[0].start()
    left_copy.start()
    flag_copies[1].start()
    flag_copies[2].start()

    y_slot = {k: (col + k * sign + NY) % NY for k in range(-4, 4)}
    x_slot = {k: (x + k * sign + NX) % NX for k in (-1, 0, 1, 2)}
    zh_slot = {0: zh, 1: (zh + 3) % NZH, 2: (zh + 1) % NZH, 3: (zh + 2) % NZH}
    y_id = {k: (row, y_slot[k], depth) for k in (1, -1)}
    x_id = {k: (zh * NX + x_slot[k], col, depth) for k in (1, -1)}
    up_id = (zh_slot[2] * NX + x, col, depth)
    down_id = (zh_slot[1] * NX + x, col, depth)
    layer_id = {k: (row, col, ((zl + k) % NZL) * 2 + core) for k in (1, 2)}
    sibling = (row, col, zl * 2 + 1 - core)
    chunk = {k: (zl + 1 + k) % NZL for k in range(CHUNKS)}

    barrier = pltpu.get_barrier_semaphore()

    def greet(friend):
        pl.semaphore_signal(barrier, inc=1, device_id=friend, device_id_type=MESH)

    def mask_left():
        for block in range(4):
            rows = pl.ds(block * BLOCK, BLOCK)
            for k in range(2):
                columns = pl.ds(k * BLOCK, BLOCK)
                keep = left_flags[k, block] > 0
                value = left_in[rows, columns]
                left_buf[col, rows, columns] = jnp.where(keep, value, jnp.zeros_like(value))

    def mask_right(step):
        for j in range(2):
            keep = right_flags[0, chunk[step] * 2 + j] > 0
            start = pl.multiple_of(chunk[step] * WIDE + j * BLOCK, BLOCK)
            value = right_in[:, pl.ds(start, BLOCK)]
            right_buf[step, row, :, pl.ds(j * BLOCK, BLOCK)] = jnp.where(keep, value, jnp.zeros_like(value))

    def copy_of(ref, send_sem, recv_sem, target, dst=None):
        return pltpu.make_async_remote_copy(
            src_ref=ref, dst_ref=ref if dst is None else dst, send_sem=send_sem, recv_sem=recv_sem,
            device_id=target, device_id_type=MESH,
        )

    def left_copy_of(hop, way, half, shift):
        slot = y_slot[-shift] if way == 0 else y_slot[shift]
        final = hop == 4 - way
        return copy_of(
            left_buf.at[slot, pl.ds(half * HALF, HALF), :], left_send,
            left_last if final else left_recv.at[hop - 1, way, half], y_id[1 if way == 0 else -1],
        )

    def own_left(half):
        left_copy_of(1, 0, half, 0).start()
        left_copy_of(1, 1, half, 0).start()

    def left_event(hop, half):
        for way in range(2):
            if hop < 4 - way:
                left_copy_of(hop, way, half, hop).wait_recv()
                left_copy_of(hop + 1, way, half, hop).start()

    def z_copy(piece, source, arrival, target):
        rows = pl.ds(piece % PARTS * (BLOCK // PARTS), BLOCK // PARTS)
        ref = right_buf.at[piece // PARTS, zh_slot[source] * NX + x, rows]
        return copy_of(ref, z_send.at[piece // PARTS], z_recv.at[piece, arrival], target)

    def up(piece):
        z_copy(piece, 0, 0, up_id).start()

    def down(piece):
        z_copy(piece, 0, 1, down_id).start()

    def z_from_before(piece):
        z_copy(piece, 1, 0, up_id).wait_recv()

        @pl.when(core == 0)
        def _():
            z_copy(piece, 1, 2, up_id).start()

        own_x(piece, 1)

    def z_from_after(piece):
        z_copy(piece, 2, 1, down_id).wait_recv()

        @pl.when(core == 1)
        def _():
            z_copy(piece, 2, 2, down_id).start()

        own_x(piece, 2)

    def z_opposite(piece):
        z_copy(piece, 3, 2, up_id).wait_recv()
        own_x(piece, 3)

    def x_copy(piece, source, shift, recv_sem, way):
        rows = pl.ds(piece % PARTS * (BLOCK // PARTS), BLOCK // PARTS)
        ref = right_buf.at[piece // PARTS, zh_slot[source] * NX + x_slot[shift], rows]
        return copy_of(ref, x_send.at[piece // PARTS], recv_sem, x_id[way])

    def own_x(piece, source=0):
        x_copy(piece, source, 0, x_recv.at[piece, source], 1).start()
        x_copy(piece, source, 0, x_last.at[piece // PARTS], -1).start()

    def x_event(piece, source):
        x_copy(piece, source, -1, x_recv.at[piece, source], 1).wait_recv()
        x_copy(piece, source, -1, x_last.at[piece // PARTS], 1).start()

    def wait_x_last(step):
        blocks = right_buf.at[step, pl.ds(0, 8)]
        copy_of(blocks, x_send.at[step], x_last.at[step], x_id[1]).wait_recv()

    def wait_left_last():
        copy_of(left_buf.at[pl.ds(0, 2)], left_send, left_last, y_id[1]).wait_recv()

    def sibling_copy(step):
        return copy_of(part.at[step, 1 - core], sib_send_sem.at[step], sib_recv_sem.at[step], sibling, sib_recv.at[step])

    def layer_copy(step):
        return copy_of(red_send.at[step], red_send_sem.at[step], red_recv_sem.at[step], layer_id[1 + step], red_recv.at[step])

    def multiply(step):
        total = None
        for k in range(NY):
            term = jnp.dot(
                left_buf[k], right_buf[step, 2 * k:2 * k + 2].reshape(2 * BLOCK, WIDE),
                preferred_element_type=jnp.float32,
            )
            total = term if total is None else total + term
        part[step, 0] = total[:, :BLOCK]
        part[step, 1] = total[:, BLOCK:]
        sibling_copy(step).start()

    def reduce_send(step):
        sibling_copy(step).wait_recv()
        red_send[step] = part[step, core] + sib_recv[step]
        layer_copy(step).start()

    actions = {
        "own_x": own_x, "own_left": own_left, "X": x_event, "L": left_event, "up": up, "down": down, "Zp": z_from_before,
        "Zm": z_from_after, "Zo": z_opposite, "x_last": wait_x_last, "left_last": wait_left_last, "M": multiply,
        "R": reduce_send,
    }

    def perform(order):
        for item in order:
            name, *numbers = item.split()
            actions[name](*map(int, numbers))

    for friend in (y_id[1], y_id[-1], x_id[1], x_id[-1], sibling):
        greet(friend)
    right_copy.wait()
    flag_copies[0].wait()
    for step in range(CHUNKS):
        mask_right(step)
    left_copy.wait()
    flag_copies[1].wait()
    flag_copies[2].wait()
    mask_left()
    for friend in (layer_id[1], layer_id[2], up_id, down_id):
        greet(friend)
    pl.semaphore_wait(barrier, 9)

    perform(ORDERS[0])

    copy_of(left_buf.at[pl.ds(0, 7)], left_send, left_last, y_id[1]).wait_send()
    for step in range(CHUNKS):
        copy_of(right_buf.at[step, pl.ds(0, 3)], z_send.at[step], z_recv.at[PARTS * step, 0], up_id).wait_send()
    for step in range(CHUNKS):
        copy_of(right_buf.at[step, pl.ds(0, 12)], x_send.at[step], x_last.at[step], x_id[1]).wait_send()
    wait_x_last(2)
    multiply(2)
    sibling_copy(0).wait_send()
    sibling_copy(1).wait_send()
    layer_copy(0).wait()
    layer_copy(1).wait()
    total = part[2, core] + red_recv[0] + red_recv[1]
    sibling_copy(2).wait()
    total = total + sib_recv[2]
    for block in range(4):
        rows = slice(block * BLOCK, (block + 1) * BLOCK)
        keep = target_flags[0, block] > 0
        value = total[rows]
        out_ref[rows, :] = jnp.where(keep, value, jnp.zeros_like(value)).astype(jnp.bfloat16)


def on_device(left_panels, right_panels, left_flags, right_flags, target_flags):
    dma = pltpu.SemaphoreType.DMA
    return pl.pallas_call(
        kernel,
        out_shape=jax.ShapeDtypeStruct((4 * BLOCK, BLOCK), jnp.bfloat16),
        in_specs=[pl.BlockSpec(memory_space=pl.ANY)] * 5,
        out_specs=pl.BlockSpec(memory_space=pltpu.VMEM),
        scratch_shapes=[
            pltpu.SMEM((2, 4), jnp.int32),
            pltpu.SMEM((1, 6), jnp.int32),
            pltpu.SMEM((1, 4), jnp.int32),
            pltpu.VMEM((4 * BLOCK, 2 * BLOCK), jnp.bfloat16),
            pltpu.VMEM((BLOCK, 6 * BLOCK), jnp.bfloat16),
            pltpu.VMEM((NY, 4 * BLOCK, 2 * BLOCK), jnp.bfloat16),
            pltpu.VMEM((CHUNKS, NX * NZH, BLOCK, WIDE), jnp.bfloat16),
            pltpu.VMEM((CHUNKS, 2, 4 * BLOCK, BLOCK), jnp.float32),
            pltpu.VMEM((CHUNKS, 4 * BLOCK, BLOCK), jnp.float32),
            pltpu.VMEM((2, 4 * BLOCK, BLOCK), jnp.float32),
            pltpu.VMEM((2, 4 * BLOCK, BLOCK), jnp.float32),
            dma((5,)),
            dma,
            dma((3, 2, 2)),
            dma,
            dma((CHUNKS,)),
            dma((CHUNKS * PARTS, 3)),
            dma((CHUNKS,)),
            dma((CHUNKS * PARTS, 4)),
            dma((CHUNKS,)),
            dma((CHUNKS,)),
            dma((CHUNKS,)),
            dma((2,)),
            dma((2,)),
        ],
        compiler_params=pltpu.CompilerParams(
            collective_id=0, has_side_effects=True, vmem_limit_bytes=VMEM_LIMIT
        ),
        cost_estimate=pl.CostEstimate(flops=1_610_612_736, bytes_accessed=600_000, transcendentals=0),
    )(left_panels[:, 0, :], right_panels[0], left_flags[:, 0, :].T, right_flags[0], target_flags.T)


VMEM_LIMIT = 63 * 1024 * 1024


def solution(mesh):
    in_specs = (
        P("row", "depth", "col"),
        P("depth", "row", "col"),
        P("row", "depth", "col"),
        P("depth", "row", "col"),
        P("row", ("col", "depth")),
    )
    out_specs = P("row", ("col", "depth"))
    return jax.shard_map(
        on_device, mesh=mesh, in_specs=in_specs, out_specs=out_specs, check_vma=False
    )
```

```python
import jax
import jax.numpy as jnp
from jax import lax
from jax.experimental import pallas as pl
from jax.experimental.pallas import tpu as pltpu
from jax.sharding import PartitionSpec as P

BLOCK = 128
MESH = pl.DeviceIdType.MESH
NX, NY, NZH, NZL = 4, 8, 4, 3
HALF = 256
WIDE = 256
CHUNKS = 3
PARTS = 2

ORDERS = (
    (
        "up 0", "down 0", "own_x 0", "own_left 0", "up 1", "down 1", "own_left 1", "own_x 1",
        "own_x 2", "own_x 3", "own_x 4", "own_x 5", "X 0 0", "X 1 0", "X 2 0", "X 3 0",
        "Zp 0", "up 2", "X 4 0", "Zm 0", "down 2", "L 1 0", "X 5 0", "Zp 1",
        "up 3", "Zm 1", "down 3", "L 1 1", "X 0 1", "X 0 2", "X 1 1", "L 2 0",
        "Zo 0", "X 1 2", "Zp 2", "Zo 1", "Zm 2", "up 4", "down 4", "X 0 3",
        "L 2 1", "Zp 3", "up 5", "Zm 3", "down 5", "X 2 1", "X 2 2", "X 1 3",
        "L 3 0", "X 3 1", "Zp 4", "Zm 4", "Zo 3", "X 3 2", "L 3 1", "Zo 2",
        "Zp 5", "X 4 1", "Zm 5", "X 4 2", "x_last 0", "X 2 3", "left_last", "M 0",
        "Zo 4", "X 5 2", "X 5 1", "X 3 3", "R 0", "x_last 1", "M 1", "X 4 3",
        "Zo 5", "X 5 3", "R 1",
    ),
)


def kernel(
    left_hbm, right_hbm, left_flags_hbm, right_flags_hbm, target_flags_hbm, out_ref,
    left_flags, right_flags, target_flags,
    left_in, right_in, left_buf, right_buf, part, sib_recv, red_send, red_recv,
    in_sem, left_send, left_recv, left_last, z_send, z_recv, x_send, x_recv, x_last,
    sib_send_sem, sib_recv_sem, red_send_sem, red_recv_sem,
):
    row, col, depth = lax.axis_index("row"), lax.axis_index("col"), lax.axis_index("depth")
    zh, x = row // NX, row % NX
    zl, core = depth // 2, depth % 2
    sign = 1 - 2 * core

    left_copy = pltpu.make_async_copy(left_hbm, left_in, in_sem.at[0])
    right_copy = pltpu.make_async_copy(right_hbm, right_in, in_sem.at[1])
    flag_copies = [
        pltpu.make_async_copy(right_flags_hbm, right_flags, in_sem.at[2]),
        pltpu.make_async_copy(left_flags_hbm, left_flags, in_sem.at[3]),
        pltpu.make_async_copy(target_flags_hbm, target_flags, in_sem.at[4]),
    ]
    right_copy.start()
    flag_copies[0].start()
    left_copy.start()
    flag_copies[1].start()
    flag_copies[2].start()

    y_slot = {k: (col + k * sign + NY) % NY for k in range(-4, 4)}
    x_slot = {k: (x + k * sign + NX) % NX for k in (-1, 0, 1, 2)}
    zh_slot = {0: zh, 1: (zh + 3) % NZH, 2: (zh + 1) % NZH, 3: (zh + 2) % NZH}
    y_id = {k: (row, y_slot[k], depth) for k in (1, -1)}
    x_id = {k: (zh * NX + x_slot[k], col, depth) for k in (1, -1)}
    up_id = (zh_slot[2] * NX + x, col, depth)
    down_id = (zh_slot[1] * NX + x, col, depth)
    layer_id = {k: (row, col, ((zl + k) % NZL) * 2 + core) for k in (1, 2)}
    sibling = (row, col, zl * 2 + 1 - core)
    chunk = {k: (zl + 1 + k) % NZL for k in range(CHUNKS)}

    barrier = pltpu.get_barrier_semaphore()

    def greet(friend):
        pl.semaphore_signal(barrier, inc=1, device_id=friend, device_id_type=MESH)

    def mask_left():
        for block in range(4):
            rows = pl.ds(block * BLOCK, BLOCK)
            for k in range(2):
                columns = pl.ds(k * BLOCK, BLOCK)
                keep = left_flags[k, block] > 0
                value = left_in[rows, columns]
                left_buf[col, rows, columns] = jnp.where(keep, value, jnp.zeros_like(value))

    def mask_right(step):
        for j in range(2):
            keep = right_flags[0, chunk[step] * 2 + j] > 0
            start = pl.multiple_of(chunk[step] * WIDE + j * BLOCK, BLOCK)
            value = right_in[:, pl.ds(start, BLOCK)]
            right_buf[step, row, :, pl.ds(j * BLOCK, BLOCK)] = jnp.where(keep, value, jnp.zeros_like(value))

    def copy_of(ref, send_sem, recv_sem, target, dst=None):
        return pltpu.make_async_remote_copy(
            src_ref=ref, dst_ref=ref if dst is None else dst, send_sem=send_sem, recv_sem=recv_sem,
            device_id=target, device_id_type=MESH,
        )

    def left_copy_of(hop, way, half, shift):
        slot = y_slot[-shift] if way == 0 else y_slot[shift]
        final = hop == 4 - way
        return copy_of(
            left_buf.at[slot, pl.ds(half * HALF, HALF), :], left_send,
            left_last if final else left_recv.at[hop - 1, way, half], y_id[1 if way == 0 else -1],
        )

    def own_left(half):
        left_copy_of(1, 0, half, 0).start()
        left_copy_of(1, 1, half, 0).start()

    def left_event(hop, half):
        for way in range(2):
            if hop < 4 - way:
                left_copy_of(hop, way, half, hop).wait_recv()
                left_copy_of(hop + 1, way, half, hop).start()

    def z_copy(piece, source, arrival, target):
        rows = pl.ds(piece % PARTS * (BLOCK // PARTS), BLOCK // PARTS)
        ref = right_buf.at[piece // PARTS, zh_slot[source] * NX + x, rows]
        return copy_of(ref, z_send.at[piece // PARTS], z_recv.at[piece, arrival], target)

    def up(piece):
        z_copy(piece, 0, 0, up_id).start()

    def down(piece):
        z_copy(piece, 0, 1, down_id).start()

    def z_from_before(piece):
        z_copy(piece, 1, 0, up_id).wait_recv()

        @pl.when(core == 0)
        def _():
            z_copy(piece, 1, 2, up_id).start()

        own_x(piece, 1)

    def z_from_after(piece):
        z_copy(piece, 2, 1, down_id).wait_recv()

        @pl.when(core == 1)
        def _():
            z_copy(piece, 2, 2, down_id).start()

        own_x(piece, 2)

    def z_opposite(piece):
        z_copy(piece, 3, 2, up_id).wait_recv()
        own_x(piece, 3)

    def x_copy(piece, source, shift, recv_sem, way):
        rows = pl.ds(piece % PARTS * (BLOCK // PARTS), BLOCK // PARTS)
        ref = right_buf.at[piece // PARTS, zh_slot[source] * NX + x_slot[shift], rows]
        return copy_of(ref, x_send.at[piece // PARTS], recv_sem, x_id[way])

    def own_x(piece, source=0):
        x_copy(piece, source, 0, x_recv.at[piece, source], 1).start()
        x_copy(piece, source, 0, x_last.at[piece // PARTS], -1).start()

    def x_event(piece, source):
        x_copy(piece, source, -1, x_recv.at[piece, source], 1).wait_recv()
        x_copy(piece, source, -1, x_last.at[piece // PARTS], 1).start()

    def wait_x_last(step):
        blocks = right_buf.at[step, pl.ds(0, 8)]
        copy_of(blocks, x_send.at[step], x_last.at[step], x_id[1]).wait_recv()

    def wait_left_last():
        copy_of(left_buf.at[pl.ds(0, 2)], left_send, left_last, y_id[1]).wait_recv()

    def sibling_copy(step):
        return copy_of(part.at[step, 1 - core], sib_send_sem.at[step], sib_recv_sem.at[step], sibling, sib_recv.at[step])

    def layer_copy(step):
        return copy_of(red_send.at[step], red_send_sem.at[step], red_recv_sem.at[step], layer_id[1 + step], red_recv.at[step])

    def multiply_whole(step):
        total = None
        for k in range(NY):
            term = jnp.dot(
                left_buf[k], right_buf[step, 2 * k:2 * k + 2].reshape(2 * BLOCK, WIDE),
                preferred_element_type=jnp.float32,
            )
            total = term if total is None else total + term
        part[step, 0] = total[:, :BLOCK]
        part[step, 1] = total[:, BLOCK:]
        sibling_copy(step).start()

    def multiply_half(step, half):
        columns = pl.ds(pl.multiple_of(half * BLOCK, BLOCK), BLOCK)
        total = None
        for k in range(NY):
            term = jnp.dot(
                left_buf[k], right_buf[step, 2 * k:2 * k + 2, :, columns].reshape(2 * BLOCK, BLOCK),
                preferred_element_type=jnp.float32,
            )
            total = term if total is None else total + term
        part[step, half] = total

    def multiply(step):
        if step < 2:
            return multiply_whole(step)
        multiply_half(step, 1 - core)
        sibling_copy(step).start()
        multiply_half(step, core)

    def reduce_send(step):
        sibling_copy(step).wait_recv()
        red_send[step] = part[step, core] + sib_recv[step]
        layer_copy(step).start()

    actions = {
        "own_x": own_x, "own_left": own_left, "X": x_event, "L": left_event, "up": up, "down": down, "Zp": z_from_before,
        "Zm": z_from_after, "Zo": z_opposite, "x_last": wait_x_last, "left_last": wait_left_last, "M": multiply,
        "R": reduce_send,
    }

    def perform(order):
        for item in order:
            name, *numbers = item.split()
            actions[name](*map(int, numbers))

    for friend in (y_id[1], y_id[-1], x_id[1], x_id[-1], sibling):
        greet(friend)
    right_copy.wait()
    flag_copies[0].wait()
    for step in range(CHUNKS):
        mask_right(step)
    left_copy.wait()
    flag_copies[1].wait()
    flag_copies[2].wait()
    mask_left()
    for friend in (layer_id[1], layer_id[2], up_id, down_id):
        greet(friend)
    pl.semaphore_wait(barrier, 9)

    perform(ORDERS[0])

    copy_of(left_buf.at[pl.ds(0, 7)], left_send, left_last, y_id[1]).wait_send()
    for step in range(CHUNKS):
        copy_of(right_buf.at[step, pl.ds(0, 3)], z_send.at[step], z_recv.at[PARTS * step, 0], up_id).wait_send()
    for step in range(CHUNKS):
        copy_of(right_buf.at[step, pl.ds(0, 12)], x_send.at[step], x_last.at[step], x_id[1]).wait_send()
    wait_x_last(2)
    multiply(2)
    sibling_copy(0).wait_send()
    sibling_copy(1).wait_send()
    layer_copy(0).wait()
    layer_copy(1).wait()
    total = part[2, core] + red_recv[0] + red_recv[1]
    sibling_copy(2).wait()
    total = total + sib_recv[2]
    for block in range(4):
        rows = slice(block * BLOCK, (block + 1) * BLOCK)
        keep = target_flags[0, block] > 0
        value = total[rows]
        out_ref[rows, :] = jnp.where(keep, value, jnp.zeros_like(value)).astype(jnp.bfloat16)


def on_device(left_panels, right_panels, left_flags, right_flags, target_flags):
    dma = pltpu.SemaphoreType.DMA
    return pl.pallas_call(
        kernel,
        out_shape=jax.ShapeDtypeStruct((4 * BLOCK, BLOCK), jnp.bfloat16),
        in_specs=[pl.BlockSpec(memory_space=pl.ANY)] * 5,
        out_specs=pl.BlockSpec(memory_space=pltpu.VMEM),
        scratch_shapes=[
            pltpu.SMEM((2, 4), jnp.int32),
            pltpu.SMEM((1, 6), jnp.int32),
            pltpu.SMEM((1, 4), jnp.int32),
            pltpu.VMEM((4 * BLOCK, 2 * BLOCK), jnp.bfloat16),
            pltpu.VMEM((BLOCK, 6 * BLOCK), jnp.bfloat16),
            pltpu.VMEM((NY, 4 * BLOCK, 2 * BLOCK), jnp.bfloat16),
            pltpu.VMEM((CHUNKS, NX * NZH, BLOCK, WIDE), jnp.bfloat16),
            pltpu.VMEM((CHUNKS, 2, 4 * BLOCK, BLOCK), jnp.float32),
            pltpu.VMEM((CHUNKS, 4 * BLOCK, BLOCK), jnp.float32),
            pltpu.VMEM((2, 4 * BLOCK, BLOCK), jnp.float32),
            pltpu.VMEM((2, 4 * BLOCK, BLOCK), jnp.float32),
            dma((5,)),
            dma,
            dma((3, 2, 2)),
            dma,
            dma((CHUNKS,)),
            dma((CHUNKS * PARTS, 3)),
            dma((CHUNKS,)),
            dma((CHUNKS * PARTS, 4)),
            dma((CHUNKS,)),
            dma((CHUNKS,)),
            dma((CHUNKS,)),
            dma((2,)),
            dma((2,)),
        ],
        compiler_params=pltpu.CompilerParams(
            collective_id=0, has_side_effects=True, vmem_limit_bytes=VMEM_LIMIT
        ),
        cost_estimate=pl.CostEstimate(flops=1_610_612_736, bytes_accessed=600_000, transcendentals=0),
    )(left_panels[:, 0, :], right_panels[0], left_flags[:, 0, :].T, right_flags[0], target_flags.T)


VMEM_LIMIT = 63 * 1024 * 1024


def solution(mesh):
    in_specs = (
        P("row", "depth", "col"),
        P("depth", "row", "col"),
        P("row", "depth", "col"),
        P("depth", "row", "col"),
        P("row", ("col", "depth")),
    )
    out_specs = P("row", ("col", "depth"))
    return jax.shard_map(
        on_device, mesh=mesh, in_specs=in_specs, out_specs=out_specs, check_vma=False
    )
```

```python
import jax
import jax.numpy as jnp
from jax import lax
from jax.experimental import pallas as pl
from jax.experimental.pallas import tpu as pltpu
from jax.sharding import PartitionSpec as P

BLOCK = 128
MESH = pl.DeviceIdType.MESH
NX, NY, NZH, NZL = 4, 8, 4, 3
HALF = 256
WIDE = 256
CHUNKS = 3
PARTS = 2

ORDERS = (
    (
        "up 0", "down 0", "own_x 0", "own_left 0", "up 1", "down 1", "own_left 1", "own_x 1",
        "own_x 2", "own_x 3", "own_x 4", "own_x 5", "X 0 0", "X 1 0", "X 2 0", "X 3 0",
        "Zp 0", "up 2", "X 4 0", "Zm 0", "down 2", "L 1 0", "X 5 0", "Zp 1",
        "up 3", "Zm 1", "down 3", "L 1 1", "X 0 1", "X 0 2", "X 1 1", "L 2 0",
        "Zo 0", "X 1 2", "Zp 2", "Zo 1", "Zm 2", "up 4", "down 4", "X 0 3",
        "L 2 1", "Zp 3", "up 5", "Zm 3", "down 5", "X 2 1", "X 2 2", "X 1 3",
        "L 3 0", "X 3 1", "Zp 4", "Zm 4", "Zo 3", "X 3 2", "L 3 1", "Zo 2",
        "Zp 5", "X 4 1", "Zm 5", "X 4 2", "x_last 0", "X 2 3", "left_last", "M 0",
        "Zo 4", "X 5 2", "X 5 1", "X 3 3", "R 0", "x_last 1", "M 1", "X 4 3",
        "Zo 5", "X 5 3", "R 1",
    ),
)


def kernel(
    left_hbm, right_hbm, left_flags_hbm, right_flags_hbm, target_flags_hbm, out_ref,
    left_flags, right_flags, target_flags,
    left_in, right_in, left_buf, right_buf, part, sib_recv, red_send, red_recv,
    in_sem, left_send, left_recv, left_last, z_send, z_recv, x_send, x_recv, x_last,
    sib_send_sem, sib_recv_sem, red_send_sem, red_recv_sem,
):
    row, col, depth = lax.axis_index("row"), lax.axis_index("col"), lax.axis_index("depth")
    zh, x = row // NX, row % NX
    zl, core = depth // 2, depth % 2
    sign = 1 - 2 * core

    left_copy = pltpu.make_async_copy(left_hbm, left_in, in_sem.at[0])
    right_copy = pltpu.make_async_copy(right_hbm, right_in, in_sem.at[1])
    flag_copies = [
        pltpu.make_async_copy(right_flags_hbm, right_flags, in_sem.at[2]),
        pltpu.make_async_copy(left_flags_hbm, left_flags, in_sem.at[3]),
        pltpu.make_async_copy(target_flags_hbm, target_flags, in_sem.at[4]),
    ]
    right_copy.start()
    flag_copies[0].start()
    left_copy.start()
    flag_copies[1].start()
    flag_copies[2].start()

    y_slot = {k: (col + k * sign + NY) % NY for k in range(-4, 4)}
    x_slot = {k: (x + k * sign + NX) % NX for k in (-1, 0, 1, 2)}
    zh_slot = {0: zh, 1: (zh + 3) % NZH, 2: (zh + 1) % NZH, 3: (zh + 2) % NZH}
    y_id = {k: (row, y_slot[k], depth) for k in (1, -1)}
    x_id = {k: (zh * NX + x_slot[k], col, depth) for k in (1, -1)}
    up_id = (zh_slot[2] * NX + x, col, depth)
    down_id = (zh_slot[1] * NX + x, col, depth)
    layer_id = {k: (row, col, ((zl + k) % NZL) * 2 + core) for k in (1, 2)}
    sibling = (row, col, zl * 2 + 1 - core)
    chunk = {k: (zl + 1 + k) % NZL for k in range(CHUNKS)}

    barrier = pltpu.get_barrier_semaphore()

    def greet(friend):
        pl.semaphore_signal(barrier, inc=1, device_id=friend, device_id_type=MESH)

    def mask_left():
        for block in range(4):
            rows = pl.ds(block * BLOCK, BLOCK)
            for k in range(2):
                columns = pl.ds(k * BLOCK, BLOCK)
                keep = left_flags[k, block] > 0
                value = left_in[rows, columns]
                left_buf[col, rows, columns] = jnp.where(keep, value, jnp.zeros_like(value))

    def mask_right(step):
        for j in range(2):
            keep = right_flags[0, chunk[step] * 2 + j] > 0
            start = pl.multiple_of(chunk[step] * WIDE + j * BLOCK, BLOCK)
            value = right_in[:, pl.ds(start, BLOCK)]
            right_buf[step, row, :, pl.ds(j * BLOCK, BLOCK)] = jnp.where(keep, value, jnp.zeros_like(value))

    def copy_of(ref, send_sem, recv_sem, target, dst=None):
        return pltpu.make_async_remote_copy(
            src_ref=ref, dst_ref=ref if dst is None else dst, send_sem=send_sem, recv_sem=recv_sem,
            device_id=target, device_id_type=MESH,
        )

    def left_copy_of(hop, way, half, shift):
        slot = y_slot[-shift] if way == 0 else y_slot[shift]
        final = hop == 4 - way
        return copy_of(
            left_buf.at[slot, pl.ds(half * HALF, HALF), :], left_send,
            left_last if final else left_recv.at[hop - 1, way, half], y_id[1 if way == 0 else -1],
        )

    def own_left(half):
        left_copy_of(1, 0, half, 0).start()
        left_copy_of(1, 1, half, 0).start()

    def left_event(hop, half):
        for way in range(2):
            if hop < 4 - way:
                left_copy_of(hop, way, half, hop).wait_recv()
                left_copy_of(hop + 1, way, half, hop).start()

    def z_copy(piece, source, arrival, target):
        rows = pl.ds(piece % PARTS * (BLOCK // PARTS), BLOCK // PARTS)
        ref = right_buf.at[piece // PARTS, zh_slot[source] * NX + x, rows]
        return copy_of(ref, z_send.at[piece // PARTS], z_recv.at[piece, arrival], target)

    def up(piece):
        z_copy(piece, 0, 0, up_id).start()

    def down(piece):
        z_copy(piece, 0, 1, down_id).start()

    def z_from_before(piece):
        z_copy(piece, 1, 0, up_id).wait_recv()

        @pl.when(core == 0)
        def _():
            z_copy(piece, 1, 2, up_id).start()

        own_x(piece, 1)

    def z_from_after(piece):
        z_copy(piece, 2, 1, down_id).wait_recv()

        @pl.when(core == 1)
        def _():
            z_copy(piece, 2, 2, down_id).start()

        own_x(piece, 2)

    def z_opposite(piece):
        z_copy(piece, 3, 2, up_id).wait_recv()
        own_x(piece, 3)

    def x_copy(piece, source, shift, recv_sem, way):
        rows = pl.ds(piece % PARTS * (BLOCK // PARTS), BLOCK // PARTS)
        ref = right_buf.at[piece // PARTS, zh_slot[source] * NX + x_slot[shift], rows]
        return copy_of(ref, x_send.at[piece // PARTS], recv_sem, x_id[way])

    def own_x(piece, source=0):
        x_copy(piece, source, 0, x_recv.at[piece, source], 1).start()
        x_copy(piece, source, 0, x_last.at[piece // PARTS], -1).start()

    def x_event(piece, source):
        x_copy(piece, source, -1, x_recv.at[piece, source], 1).wait_recv()
        x_copy(piece, source, -1, x_last.at[piece // PARTS], 1).start()

    def wait_x_last(step):
        blocks = right_buf.at[step, pl.ds(0, 8)]
        copy_of(blocks, x_send.at[step], x_last.at[step], x_id[1]).wait_recv()

    def wait_left_last():
        copy_of(left_buf.at[pl.ds(0, 2)], left_send, left_last, y_id[1]).wait_recv()

    def sibling_copy(step):
        return copy_of(part.at[step, 1 - core], sib_send_sem.at[step], sib_recv_sem.at[step], sibling, sib_recv.at[step])

    def layer_copy(step):
        return copy_of(red_send.at[step], red_send_sem.at[step], red_recv_sem.at[step], layer_id[1 + step], red_recv.at[step])

    def multiply(step):
        total = None
        for k in range(NY):
            term = jnp.dot(
                left_buf[k], right_buf[step, 2 * k:2 * k + 2].reshape(2 * BLOCK, WIDE),
                preferred_element_type=jnp.float32,
            )
            total = term if total is None else total + term
        part[step, 0] = total[:, :BLOCK]
        part[step, 1] = total[:, BLOCK:]
        sibling_copy(step).start()

    def reduce_send(step):
        sibling_copy(step).wait_recv()
        red_send[step] = part[step, core] + sib_recv[step]
        layer_copy(step).start()

    actions = {
        "own_x": own_x, "own_left": own_left, "X": x_event, "L": left_event, "up": up, "down": down, "Zp": z_from_before,
        "Zm": z_from_after, "Zo": z_opposite, "x_last": wait_x_last, "left_last": wait_left_last, "M": multiply,
        "R": reduce_send,
    }

    def perform(order):
        for item in order:
            name, *numbers = item.split()
            actions[name](*map(int, numbers))

    for friend in (y_id[1], y_id[-1], x_id[1], x_id[-1], sibling):
        greet(friend)
    right_copy.wait()
    flag_copies[0].wait()
    for step in range(CHUNKS):
        mask_right(step)
    left_copy.wait()
    flag_copies[1].wait()
    flag_copies[2].wait()
    mask_left()
    for friend in (layer_id[1], layer_id[2], up_id, down_id):
        greet(friend)
    pl.semaphore_wait(barrier, 9)

    perform(ORDERS[0])

    copy_of(left_buf.at[pl.ds(0, 7)], left_send, left_last, y_id[1]).wait_send()
    for step in range(CHUNKS):
        copy_of(right_buf.at[step, pl.ds(0, 3)], z_send.at[step], z_recv.at[PARTS * step, 0], up_id).wait_send()
    for step in range(CHUNKS):
        copy_of(right_buf.at[step, pl.ds(0, 12)], x_send.at[step], x_last.at[step], x_id[1]).wait_send()
    wait_x_last(2)
    multiply(2)
    sibling_copy(0).wait_send()
    sibling_copy(1).wait_send()
    layer_copy(0).wait()
    layer_copy(1).wait()
    total = part[2, core] + red_recv[0] + red_recv[1]
    sibling_copy(2).wait()
    total = total + sib_recv[2]
    for block in range(4):
        rows = slice(block * BLOCK, (block + 1) * BLOCK)
        keep = target_flags[0, block] > 0
        value = total[rows]
        out_ref[rows, :] = jnp.where(keep, value, jnp.zeros_like(value)).astype(jnp.bfloat16)


def on_device(left_panels, right_panels, left_flags, right_flags, target_flags):
    dma = pltpu.SemaphoreType.DMA
    return pl.pallas_call(
        kernel,
        out_shape=jax.ShapeDtypeStruct((4 * BLOCK, BLOCK), jnp.bfloat16),
        in_specs=[pl.BlockSpec(memory_space=pl.ANY)] * 5,
        out_specs=pl.BlockSpec(memory_space=pltpu.VMEM),
        scratch_shapes=[
            pltpu.SMEM((2, 4), jnp.int32),
            pltpu.SMEM((1, 6), jnp.int32),
            pltpu.SMEM((1, 4), jnp.int32),
            pltpu.VMEM((4 * BLOCK, 2 * BLOCK), jnp.bfloat16),
            pltpu.VMEM((BLOCK, 6 * BLOCK), jnp.bfloat16),
            pltpu.VMEM((NY, 4 * BLOCK, 2 * BLOCK), jnp.bfloat16),
            pltpu.VMEM((CHUNKS, NX * NZH, BLOCK, WIDE), jnp.bfloat16),
            pltpu.VMEM((CHUNKS, 2, 4 * BLOCK, BLOCK), jnp.float32),
            pltpu.VMEM((CHUNKS, 4 * BLOCK, BLOCK), jnp.float32),
            pltpu.VMEM((2, 4 * BLOCK, BLOCK), jnp.float32),
            pltpu.VMEM((2, 4 * BLOCK, BLOCK), jnp.float32),
            dma((5,)),
            dma,
            dma((3, 2, 2)),
            dma,
            dma((CHUNKS,)),
            dma((CHUNKS * PARTS, 3)),
            dma((CHUNKS,)),
            dma((CHUNKS * PARTS, 4)),
            dma((CHUNKS,)),
            dma((CHUNKS,)),
            dma((CHUNKS,)),
            dma((2,)),
            dma((2,)),
        ],
        compiler_params=pltpu.CompilerParams(
            collective_id=0, has_side_effects=True, vmem_limit_bytes=VMEM_LIMIT
        ),
        cost_estimate=pl.CostEstimate(flops=1_610_612_736, bytes_accessed=600_000, transcendentals=0),
    )(left_panels[:, 0, :], right_panels[0], left_flags[:, 0, :].T, right_flags[0], target_flags.T)


VMEM_LIMIT = 63 * 1024 * 1024


def solution(mesh):
    in_specs = (
        P("row", "depth", "col"),
        P("depth", "row", "col"),
        P("row", "depth", "col"),
        P("depth", "row", "col"),
        P("row", ("col", "depth")),
    )
    out_specs = P("row", ("col", "depth"))
    return jax.shard_map(
        on_device, mesh=mesh, in_specs=in_specs, out_specs=out_specs, check_vma=False
    )
```

```python
import jax
import jax.numpy as jnp
from jax import lax
from jax.experimental import pallas as pl
from jax.experimental.pallas import tpu as pltpu
from jax.sharding import PartitionSpec as P

BLOCK = 128
MESH = pl.DeviceIdType.MESH
NX, NY, NZH, NZL = 4, 8, 4, 3
HALF = 256
WIDE = 256
CHUNKS = 3
PARTS = 2

ORDERS = (
    (
        "up 0", "down 0", "own_x 0", "up 1", "down 1", "own_x 1", "ready_left", "own_left 0",
        "own_left 1", "ready_right", "own_x 2", "own_x 3", "own_x 4", "own_x 5", "X 0 0", "X 1 0",
        "X 2 0", "X 3 0", "Zp 0", "up 2", "X 4 0", "Zm 0", "down 2", "L 1 0",
        "X 5 0", "Zp 1", "up 3", "Zm 1", "down 3", "L 1 1", "X 0 1", "X 0 2",
        "X 1 1", "L 2 0", "Zo 0", "X 1 2", "Zp 2", "Zo 1", "Zm 2", "up 4",
        "down 4", "X 0 3", "L 2 1", "Zp 3", "up 5", "Zm 3", "down 5", "X 2 1",
        "X 2 2", "X 1 3", "L 3 0", "X 3 1", "Zp 4", "Zm 4", "Zo 3", "X 3 2",
        "L 3 1", "Zo 2", "Zp 5", "X 4 1", "Zm 5", "X 4 2", "x_last 0", "X 2 3",
        "left_last", "M 0", "Zo 4", "X 5 2", "X 5 1", "X 3 3", "R 0", "x_last 1",
        "M 1", "X 4 3", "Zo 5", "X 5 3", "R 1",
    ),
)


def kernel(
    left_hbm, right_hbm, left_flags_hbm, right_flags_hbm, target_flags_hbm, out_ref,
    left_flags, right_flags, target_flags,
    left_in, right_in, left_buf, right_buf, part, sib_recv, red_send, red_recv,
    in_sem, left_send, left_recv, left_last, z_send, z_recv, x_send, x_recv, x_last,
    sib_send_sem, sib_recv_sem, red_send_sem, red_recv_sem,
):
    row, col, depth = lax.axis_index("row"), lax.axis_index("col"), lax.axis_index("depth")
    zh, x = row // NX, row % NX
    zl, core = depth // 2, depth % 2
    sign = 1 - 2 * core

    left_copy = pltpu.make_async_copy(left_hbm, left_in, in_sem.at[0])
    right_copy = pltpu.make_async_copy(right_hbm, right_in, in_sem.at[1])
    flag_copies = [
        pltpu.make_async_copy(right_flags_hbm, right_flags, in_sem.at[2]),
        pltpu.make_async_copy(left_flags_hbm, left_flags, in_sem.at[3]),
        pltpu.make_async_copy(target_flags_hbm, target_flags, in_sem.at[4]),
    ]
    right_copy.start()
    flag_copies[0].start()
    left_copy.start()
    flag_copies[1].start()
    flag_copies[2].start()

    y_slot = {k: (col + k * sign + NY) % NY for k in range(-4, 4)}
    x_slot = {k: (x + k * sign + NX) % NX for k in (-1, 0, 1, 2)}
    zh_slot = {0: zh, 1: (zh + 3) % NZH, 2: (zh + 1) % NZH, 3: (zh + 2) % NZH}
    y_id = {k: (row, y_slot[k], depth) for k in (1, -1)}
    x_id = {k: (zh * NX + x_slot[k], col, depth) for k in (1, -1)}
    up_id = (zh_slot[2] * NX + x, col, depth)
    down_id = (zh_slot[1] * NX + x, col, depth)
    layer_id = {k: (row, col, ((zl + k) % NZL) * 2 + core) for k in (1, 2)}
    sibling = (row, col, zl * 2 + 1 - core)
    chunk = {k: (zl + 1 + k) % NZL for k in range(CHUNKS)}

    barrier = pltpu.get_barrier_semaphore()

    def greet(friend):
        pl.semaphore_signal(barrier, inc=1, device_id=friend, device_id_type=MESH)

    def mask_left():
        for block in range(4):
            rows = pl.ds(block * BLOCK, BLOCK)
            for k in range(2):
                columns = pl.ds(k * BLOCK, BLOCK)
                keep = left_flags[k, block] > 0
                value = left_in[rows, columns]
                left_buf[col, rows, columns] = jnp.where(keep, value, jnp.zeros_like(value))

    def mask_right(step):
        for j in range(2):
            keep = right_flags[0, chunk[step] * 2 + j] > 0
            start = pl.multiple_of(chunk[step] * WIDE + j * BLOCK, BLOCK)
            value = right_in[:, pl.ds(start, BLOCK)]
            right_buf[step, row, :, pl.ds(j * BLOCK, BLOCK)] = jnp.where(keep, value, jnp.zeros_like(value))

    def copy_of(ref, send_sem, recv_sem, target, dst=None):
        return pltpu.make_async_remote_copy(
            src_ref=ref, dst_ref=ref if dst is None else dst, send_sem=send_sem, recv_sem=recv_sem,
            device_id=target, device_id_type=MESH,
        )

    def left_copy_of(hop, way, half, shift):
        slot = y_slot[-shift] if way == 0 else y_slot[shift]
        final = hop == 4 - way
        return copy_of(
            left_buf.at[slot, pl.ds(half * HALF, HALF), :], left_send,
            left_last if final else left_recv.at[hop - 1, way, half], y_id[1 if way == 0 else -1],
        )

    def own_left(half):
        left_copy_of(1, 0, half, 0).start()
        left_copy_of(1, 1, half, 0).start()

    def left_event(hop, half):
        for way in range(2):
            if hop < 4 - way:
                left_copy_of(hop, way, half, hop).wait_recv()
                left_copy_of(hop + 1, way, half, hop).start()

    def z_copy(piece, source, arrival, target):
        rows = pl.ds(piece % PARTS * (BLOCK // PARTS), BLOCK // PARTS)
        ref = right_buf.at[piece // PARTS, zh_slot[source] * NX + x, rows]
        return copy_of(ref, z_send.at[piece // PARTS], z_recv.at[piece, arrival], target)

    def up(piece):
        z_copy(piece, 0, 0, up_id).start()

    def down(piece):
        z_copy(piece, 0, 1, down_id).start()

    def z_from_before(piece):
        z_copy(piece, 1, 0, up_id).wait_recv()

        @pl.when(core == 0)
        def _():
            z_copy(piece, 1, 2, up_id).start()

        own_x(piece, 1)

    def z_from_after(piece):
        z_copy(piece, 2, 1, down_id).wait_recv()

        @pl.when(core == 1)
        def _():
            z_copy(piece, 2, 2, down_id).start()

        own_x(piece, 2)

    def z_opposite(piece):
        z_copy(piece, 3, 2, up_id).wait_recv()
        own_x(piece, 3)

    def x_copy(piece, source, shift, recv_sem, way):
        rows = pl.ds(piece % PARTS * (BLOCK // PARTS), BLOCK // PARTS)
        ref = right_buf.at[piece // PARTS, zh_slot[source] * NX + x_slot[shift], rows]
        return copy_of(ref, x_send.at[piece // PARTS], recv_sem, x_id[way])

    def own_x(piece, source=0):
        x_copy(piece, source, 0, x_recv.at[piece, source], 1).start()
        x_copy(piece, source, 0, x_last.at[piece // PARTS], -1).start()

    def x_event(piece, source):
        x_copy(piece, source, -1, x_recv.at[piece, source], 1).wait_recv()
        x_copy(piece, source, -1, x_last.at[piece // PARTS], 1).start()

    def wait_x_last(step):
        blocks = right_buf.at[step, pl.ds(0, 8)]
        copy_of(blocks, x_send.at[step], x_last.at[step], x_id[1]).wait_recv()

    def wait_left_last():
        copy_of(left_buf.at[pl.ds(0, 2)], left_send, left_last, y_id[1]).wait_recv()

    def sibling_copy(step):
        return copy_of(part.at[step, 1 - core], sib_send_sem.at[step], sib_recv_sem.at[step], sibling, sib_recv.at[step])

    def layer_copy(step):
        return copy_of(red_send.at[step], red_send_sem.at[step], red_recv_sem.at[step], layer_id[1 + step], red_recv.at[step])

    def multiply(step):
        total = None
        for k in range(NY):
            term = jnp.dot(
                left_buf[k], right_buf[step, 2 * k:2 * k + 2].reshape(2 * BLOCK, WIDE),
                preferred_element_type=jnp.float32,
            )
            total = term if total is None else total + term
        part[step, 0] = total[:, :BLOCK]
        part[step, 1] = total[:, BLOCK:]
        sibling_copy(step).start()

    def reduce_send(step):
        sibling_copy(step).wait_recv()
        red_send[step] = part[step, core] + sib_recv[step]
        layer_copy(step).start()

    def ready_left():
        left_copy.wait()
        flag_copies[1].wait()
        flag_copies[2].wait()
        mask_left()

    def ready_right():
        for step in range(1, CHUNKS):
            mask_right(step)

    actions = {
        "ready_left": ready_left, "ready_right": ready_right,
        "own_x": own_x, "own_left": own_left, "X": x_event, "L": left_event, "up": up, "down": down, "Zp": z_from_before,
        "Zm": z_from_after, "Zo": z_opposite, "x_last": wait_x_last, "left_last": wait_left_last, "M": multiply,
        "R": reduce_send,
    }

    def perform(order):
        for item in order:
            name, *numbers = item.split()
            actions[name](*map(int, numbers))

    for friend in (y_id[1], y_id[-1], x_id[1], x_id[-1], sibling):
        greet(friend)
    right_copy.wait()
    flag_copies[0].wait()
    mask_right(0)
    for friend in (layer_id[1], layer_id[2], up_id, down_id):
        greet(friend)
    pl.semaphore_wait(barrier, 9)

    perform(ORDERS[0])

    copy_of(left_buf.at[pl.ds(0, 7)], left_send, left_last, y_id[1]).wait_send()
    for step in range(CHUNKS):
        copy_of(right_buf.at[step, pl.ds(0, 3)], z_send.at[step], z_recv.at[PARTS * step, 0], up_id).wait_send()
    for step in range(CHUNKS):
        copy_of(right_buf.at[step, pl.ds(0, 12)], x_send.at[step], x_last.at[step], x_id[1]).wait_send()
    wait_x_last(2)
    multiply(2)
    sibling_copy(0).wait_send()
    sibling_copy(1).wait_send()
    layer_copy(0).wait()
    layer_copy(1).wait()
    total = part[2, core] + red_recv[0] + red_recv[1]
    sibling_copy(2).wait()
    total = total + sib_recv[2]
    for block in range(4):
        rows = slice(block * BLOCK, (block + 1) * BLOCK)
        keep = target_flags[0, block] > 0
        value = total[rows]
        out_ref[rows, :] = jnp.where(keep, value, jnp.zeros_like(value)).astype(jnp.bfloat16)


def on_device(left_panels, right_panels, left_flags, right_flags, target_flags):
    dma = pltpu.SemaphoreType.DMA
    return pl.pallas_call(
        kernel,
        out_shape=jax.ShapeDtypeStruct((4 * BLOCK, BLOCK), jnp.bfloat16),
        in_specs=[pl.BlockSpec(memory_space=pl.ANY)] * 5,
        out_specs=pl.BlockSpec(memory_space=pltpu.VMEM),
        scratch_shapes=[
            pltpu.SMEM((2, 4), jnp.int32),
            pltpu.SMEM((1, 6), jnp.int32),
            pltpu.SMEM((1, 4), jnp.int32),
            pltpu.VMEM((4 * BLOCK, 2 * BLOCK), jnp.bfloat16),
            pltpu.VMEM((BLOCK, 6 * BLOCK), jnp.bfloat16),
            pltpu.VMEM((NY, 4 * BLOCK, 2 * BLOCK), jnp.bfloat16),
            pltpu.VMEM((CHUNKS, NX * NZH, BLOCK, WIDE), jnp.bfloat16),
            pltpu.VMEM((CHUNKS, 2, 4 * BLOCK, BLOCK), jnp.float32),
            pltpu.VMEM((CHUNKS, 4 * BLOCK, BLOCK), jnp.float32),
            pltpu.VMEM((2, 4 * BLOCK, BLOCK), jnp.float32),
            pltpu.VMEM((2, 4 * BLOCK, BLOCK), jnp.float32),
            dma((5,)),
            dma,
            dma((3, 2, 2)),
            dma,
            dma((CHUNKS,)),
            dma((CHUNKS * PARTS, 3)),
            dma((CHUNKS,)),
            dma((CHUNKS * PARTS, 4)),
            dma((CHUNKS,)),
            dma((CHUNKS,)),
            dma((CHUNKS,)),
            dma((2,)),
            dma((2,)),
        ],
        compiler_params=pltpu.CompilerParams(
            collective_id=0, has_side_effects=True, vmem_limit_bytes=VMEM_LIMIT
        ),
        cost_estimate=pl.CostEstimate(flops=1_610_612_736, bytes_accessed=600_000, transcendentals=0),
    )(left_panels[:, 0, :], right_panels[0], left_flags[:, 0, :].T, right_flags[0], target_flags.T)


VMEM_LIMIT = 63 * 1024 * 1024


def solution(mesh):
    in_specs = (
        P("row", "depth", "col"),
        P("depth", "row", "col"),
        P("row", "depth", "col"),
        P("depth", "row", "col"),
        P("row", ("col", "depth")),
    )
    out_specs = P("row", ("col", "depth"))
    return jax.shard_map(
        on_device, mesh=mesh, in_specs=in_specs, out_specs=out_specs, check_vma=False
    )
```
